32 devices in a mesh: groups: 2 (over y), col: 4 (over z), row: 4 (over x, core).
Axes of the slice: x: 2, y: 2, z: 4, core: 2. Of those that a mesh axis runs over, the one named last changes fastest.
Arguments:
- p_blocks: float32 [8, 256, 4096], P(('groups', 'col'), 'row'), parts along dimension 0, may hold values from -0.72 to 0.72
- products: int32 [8, 4, 3, 2048], P(('groups', 'col'), 'row'), parts along dimension 0, may hold values from 0 to 255, as said below
Outputs:
- square_blocks: float32 [8, 32, 4096], P(('groups', 'row'), 'col'), parts along dimension 0
The draws below stay inside these ranges and needn't reach their ends.
There are 2 independent parts, one for each index of `groups`. The reference program is written for one: setup_inputs(seed, part) draws one part's arguments, and reference() takes and returns one part's arrays. A program takes and returns all parts, laid end to end along the dimension named above; each array names one. Nothing has to cross between parts.
Inputs may be any that keep to these rules, and one draw needn't show every extreme that they name: `products`: in each list, first lies below 256, second below 64, target at most 32. Live entries (target below 32) stand before all padding entries, which are (255, 63, 32). Every list has at least one live entry; one grid cell of each part has all 2048 entries live.
All inputs are finite; a program needn't handle non-finite values.
Results may differ from the reference program's by a relative error of at most 0.0001.
Values sent between devices are 32-bit elements; how exact they have to be, the bound alone decides.
No kernel may reach another device: no remote copies, remote signals or barrier semaphores. Data moves between devices by JAX's collectives and lax.ppermute only.
A program may use at most 192 MiB of HBM per device.

```python
import jax
import jax.numpy as jnp
from jax import lax

BLK = 64
BB = 4096
S = 64
SC = 8
TILE = 128
NBAT = 16
N_COL = 4
N_ROW = 4


def draw_products(key, part):
    key = jax.random.fold_in(key, 11)
    streams = jax.random.split(key, 6)
    cells = N_COL * N_ROW
    length = NBAT * TILE
    rolls = jax.random.randint(streams[0], (cells,), 1, NBAT + 1)
    batches = jnp.maximum(1, rolls * rolls // NBAT)
    fullest = jax.random.randint(streams[1], (), 0, cells)
    shortfall = jax.random.randint(streams[2], (cells,), 0, TILE)
    positions = jnp.arange(cells)
    live_count = jnp.where(positions == fullest, length, batches * TILE - shortfall)
    first = jax.random.randint(streams[3], (cells, length), 0, N_ROW * S)
    second = jax.random.randint(streams[4], (cells, length), 0, S)
    target = jax.random.randint(streams[5], (cells, length), 0, N_COL * SC)
    used = jnp.arange(length)[None, :] < live_count[:, None]
    first = jnp.where(used, first, N_ROW * S - 1)
    second = jnp.where(used, second, S - 1)
    target = jnp.where(used, target, N_COL * SC)
    stacked = jnp.stack([first, second, target], axis=1)
    return stacked.reshape(N_COL, N_ROW, 3, length).astype(jnp.int32)


def levels(key, extent, cuts, smallest, high):
    def one(dim, blocks):
        heights = jax.random.uniform(jax.random.fold_in(jax.random.fold_in(key, 6), dim), (blocks,), jnp.float32, smallest / len(cuts), high / len(cuts))
        return jnp.repeat(jnp.exp(heights), extent[dim] // blocks).reshape((-1,) + (1,) * (len(extent) - dim - 1))

    gain = one(*cuts[0])
    for cut in cuts[1:]:
        gain = gain * one(*cut)
    return gain


def bell_draw(rng, dims, spread, most, cuts=(), kind=jnp.bfloat16):
    drawn = spread * jax.random.normal(rng, dims, jnp.float32)
    if cuts:
        drawn = drawn * levels(rng, dims, cuts, -0.22, 0.18)
    return jnp.clip(drawn, -most, most).astype(kind)


def setup_inputs(seed: int = 0, part: int = 0) -> dict:
    streams_of = jax.random.split(jax.random.key(seed), 3)
    part_keys = jax.random.split(jax.random.fold_in(streams_of[2], part), 3)
    p_blocks = bell_draw(part_keys[0], (N_COL, N_ROW * S, BB), 0.12, 0.72, ((0, 4), (1, 4)), jnp.float32)
    products = draw_products(jax.random.fold_in(jax.random.fold_in(streams_of[2], part), 71), part)
    return {"p_blocks": p_blocks, "products": products}


def batch_product(row_panel, own_blocks, product_list, number, partial_sums):
    chosen = lax.dynamic_slice_in_dim(product_list, number * TILE, TILE, 1)
    left = jnp.take(row_panel, chosen[0], axis=0).reshape(TILE, BLK, BLK)
    right = jnp.take(own_blocks, chosen[1], axis=0).reshape(TILE, BLK, BLK)
    result = jnp.einsum("nki,nkj->nij", left, right, precision=lax.Precision.HIGHEST)
    return partial_sums.at[chosen[2]].add(result.reshape(TILE, BB), mode="drop")


def device_term(row_panel, own_blocks, product_list):
    start_sums = jnp.zeros((N_COL * SC, BB), jnp.float32)

    def advance(number, partial_sums):
        return batch_product(row_panel, own_blocks, product_list, number, partial_sums)

    return lax.fori_loop(0, NBAT, advance, start_sums)


def reference(p_blocks, products):
    grid_blocks = p_blocks.reshape(N_COL, N_ROW, S, BB)

    def column_step(summed, column_inputs):
        column_blocks, column_lists = column_inputs
        row_panel = column_blocks.reshape(N_ROW * S, BB)

        def one_cell(cell_inputs):
            return device_term(row_panel, cell_inputs[0], cell_inputs[1])

        cell_terms = lax.map(one_cell, (column_blocks, column_lists))
        return summed + cell_terms, None

    start_value = jnp.zeros((N_ROW, N_COL * SC, BB), jnp.float32)
    summed, unused = lax.scan(column_step, start_value, (grid_blocks, products))
    return summed
```

```python
import functools

import jax
import jax.numpy as jnp
from jax import lax
from jax.experimental import pallas as pl
from jax.experimental.pallas import tpu as pltpu
from jax.sharding import PartitionSpec as P

BLK = 64
BB = 4096
SC = 8
HALF = 32
LANES = 128
GROUP = 4
UNROLL = 8
CHUNKS = (32, 32)
HEAD = 128
MIB = 1 << 20


def rows_view(blocks):
    count = blocks.shape[0]
    tiles = blocks.reshape(count // 8, 8, HALF, LANES)
    return tiles.transpose(0, 2, 1, 3).reshape(count * HALF, LANES)


def blocks_view(rows):
    count = rows.shape[0] // HALF
    tiles = rows.reshape(count // 8, HALF, 8, LANES)
    return tiles.transpose(0, 2, 1, 3).reshape(count, BB)


def block_rows(ref, slot):
    start = (slot // 8) * (8 * HALF) + slot % 8
    return ref[pl.ds(start, HALF, stride=8), :]


def high_low(rows):
    high = rows.astype(jnp.bfloat16)
    low = (rows - high.astype(jnp.float32)).astype(jnp.bfloat16)
    return high, low


def fill_right(source, right, first_block, count):
    def one(slot, carry):
        high, low = high_low(block_rows(source, slot))
        at = pl.ds(pl.multiple_of((first_block + slot) * HALF, HALF), HALF)
        right[at, :LANES] = high
        right[at, LANES:] = low
        return carry

    lax.fori_loop(0, count, one, 0, unroll=8)


def fill_left(source, left, count):
    def one(slot, carry):
        high, low = high_low(block_rows(source, slot))
        high, low = high.astype(jnp.float32), low.astype(jnp.float32)
        turned = jnp.concatenate([high, low, high, low], axis=0).T
        at = pl.ds(pl.multiple_of(slot * LANES, LANES), LANES)
        left[at, :] = turned.astype(jnp.bfloat16)
        return carry

    lax.fori_loop(0, count, one, 0, unroll=2)
    left[pl.ds(count * LANES, LANES), :] = jnp.zeros((LANES, LANES), jnp.bfloat16)


def run_groups(meta, phase, code_at, empty, left, right, sums):
    begin, end = meta[phase], meta[phase + 1]
    near = lax.broadcasted_iota(jnp.int32, (LANES, LANES), 1) < BLK

    def step(number, carry):
        for inner in range(UNROLL):
            place = begin + number * UNROLL + inner
            group = meta[HEAD + place]
            base = group >> 11
            live = jnp.where(place < end, (group >> 8) & 7, 0)
            target = group & 255
            lefts, rights = [], []
            for item in range(GROUP):
                code = meta[code_at + base + item]
                own = jnp.where(item < live, code & 63, empty)
                other = jnp.where(item < live, (code >> 6) & 127, 0)
                lefts.append(left[pl.ds(pl.multiple_of(own * LANES, LANES), LANES), :])
                block = right[pl.ds(pl.multiple_of(other * HALF, HALF), HALF), :]
                rights += [block, block]
            stacked = jnp.concatenate(
                [jnp.where(near, lefts[0], lefts[1]), jnp.where(near, lefts[2], lefts[3])],
                axis=1,
            )
            term = jnp.dot(
                stacked, jnp.concatenate(rights, axis=0), preferred_element_type=jnp.float32
            )
            at = pl.ds(pl.multiple_of(target * LANES, LANES), LANES)
            sums[at, :] += term[:, :LANES] + term[:, LANES:]
        return carry

    lax.fori_loop(0, (end - begin + UNROLL - 1) // UNROLL, step, 0)


def clear(sums):
    def one(number, carry):
        at = pl.ds(pl.multiple_of(number * LANES, LANES), LANES)
        sums[at, :] = jnp.zeros((LANES, LANES), jnp.float32)
        return carry

    lax.fori_loop(0, sums.shape[0] // LANES, one, 0, unroll=2)


def pack_pairs(sums, earlier, outs):
    near = lax.broadcasted_iota(jnp.int32, (BLK, LANES), 1) < BLK
    for turn, out in enumerate(outs):
        for pair in range(SC // 2):
            at = (turn * SC + 2 * pair) * LANES
            upper0 = sums[at : at + BLK, :]
            lower0 = sums[at + BLK : at + LANES, :]
            upper1 = sums[at + LANES : at + LANES + BLK, :]
            lower1 = sums[at + LANES + BLK : at + 2 * LANES, :]
            one = upper0 + pltpu.roll(lower0, BLK, 1)
            two = pltpu.roll(upper1, BLK, 1) + lower1
            both = jnp.where(near, one, two)
            if earlier is not None:
                both = both + earlier[turn][pair]
            out[pair] = both


def near_kernel(turns, code_at, meta, own, sibling, left, *rest):
    outs, (right, sums) = rest[:turns], rest[turns:]
    count = own.shape[0] // HALF
    fill_left(own, left, count)
    fill_right(own, right, 0, count)
    fill_right(sibling, right, count, count)
    clear(sums)
    run_groups(meta, 0, code_at, count, left, right, sums)
    pack_pairs(sums, None, outs)


def far_kernel(turns, code_at, phase, meta, straight, crossed, left, *rest):
    earlier, outs, (right, sums) = rest[:turns], rest[turns : 2 * turns], rest[2 * turns :]
    count = straight.shape[0] // HALF
    fill_right(straight, right, 0, count)
    fill_right(crossed, right, count, count)
    clear(sums)
    empty = left.shape[0] // LANES - 1
    run_groups(meta, phase, code_at, empty, left, right, sums)
    pack_pairs(sums, earlier, outs)


def last_kernel(*refs):
    parts, out, turned = refs[:-2], refs[-2], refs[-1]
    for pair in range(SC // 2):
        total = parts[0][pair]
        for part in parts[1:]:
            total = total + part[pair]
        turned[:, :BLK] = total.T
        even = turned[pl.ds(0, BLK, stride=2), :]
        odd = turned[pl.ds(1, BLK, stride=2), :]
        near = lax.broadcasted_iota(jnp.int32, (BLK, LANES), 1) < BLK
        packed = jnp.where(near, even, pltpu.roll(odd, BLK, 1))
        out[pl.ds(2 * pair, HALF, stride=8), :] = packed[:HALF]
        out[pl.ds(2 * pair + 1, HALF, stride=8), :] = packed[HALF:]


def plan(lists, slots, row, col, columns, chips):
    first, second, target = lists[0], lists[1], lists[2]
    entries = first.shape[0]
    targets = columns * SC
    phases = 1 + (chips - 1) * len(CHUNKS)
    shard, slot = first // slots, first % slots
    hop = (shard // 2 - row // 2) % chips
    crossed = (shard ^ row) & 1
    chunk = jnp.zeros_like(slot)
    start = jnp.zeros_like(slot)
    size = jnp.full_like(slot, CHUNKS[0])
    at = 0
    for number, width in enumerate(CHUNKS):
        inside = slot >= at
        chunk = jnp.where(inside, number, chunk)
        start = jnp.where(inside, at, start)
        size = jnp.where(inside, width, size)
        at += width
    close = hop == 0
    phase = jnp.where(close, 0, 1 + (hop - 1) * len(CHUNKS) + chunk)
    panel_slot = jnp.where(close, crossed * slots + slot, crossed * size + slot - start)
    turn = (target // SC - col) % columns
    segments = phases * targets
    segment = jnp.where(target < targets, phase * targets + turn * SC + target % SC, segments)
    codes = lax.sort((segment << 13) | (panel_slot << 6) | second)

    edges = jnp.arange(segments + 1)
    sorted_segment = codes >> 13
    starts = jnp.sum((sorted_segment[None, :] < edges[:, None]).astype(jnp.int32), axis=1)
    live = starts[1:] - starts[:-1]
    groups = (live + GROUP - 1) // GROUP
    upto = edges[:-1][None, :] < edges[:, None]
    group_starts = jnp.sum(jnp.where(upto, groups[None, :], 0), axis=1)

    places = -(-(entries // GROUP + segments + UNROLL) // LANES) * LANES
    place = jnp.arange(places)
    passed = group_starts[1:][None, :] <= place[:, None]
    shift = starts - GROUP * group_starts
    in_segment = jnp.sum(passed.astype(jnp.int32), axis=1)
    offset = shift[0] + jnp.sum(jnp.where(passed, (shift[1:] - shift[:-1])[None, :], 0), axis=1)
    stops = jnp.concatenate([starts[1:], starts[-1:]])
    stop = stops[0] + jnp.sum(jnp.where(passed, (stops[1:] - stops[:-1])[None, :], 0), axis=1)
    base = jnp.clip(GROUP * place + offset, 0, entries)
    valid = jnp.clip(stop - base, 0, GROUP)
    described = (base << 11) | (valid << 8) | (in_segment % targets)

    bounds = group_starts[::targets]
    meta = jnp.concatenate(
        [
            jnp.pad(bounds, (0, HEAD - bounds.shape[0])),
            described,
            codes,
            jnp.zeros((LANES,), jnp.int32),
        ]
    )
    return meta, HEAD + places


def per_device(columns, rows, p_blocks, products):
    own_blocks = p_blocks[0]
    slots = own_blocks.shape[0]
    chips = rows // 2
    targets = columns * SC
    row, col = lax.axis_index("row"), lax.axis_index("col")
    swap = [(device, device ^ 1) for device in range(rows)]

    far = []
    for hop in range(1, chips):
        jump = [((device + 2 * hop) % rows, device) for device in range(rows)]
        at = 0
        for width in CHUNKS:
            piece = own_blocks[at : at + width]
            at += width
            straight = lax.ppermute(piece, "row", jump)
            far.append((straight, lax.ppermute(straight, "row", swap)))
    sibling = lax.ppermute(own_blocks, "row", swap)

    meta, code_at = plan(products[0, 0], slots, row, col, columns, chips)
    smem = pl.BlockSpec(memory_space=pltpu.SMEM)
    vmem = pl.BlockSpec(memory_space=pltpu.VMEM)
    part = jax.ShapeDtypeStruct((SC // 2, BLK, LANES), jnp.float32)
    sums_size = targets * LANES * LANES * 4
    left_shape = jax.ShapeDtypeStruct(((slots + 1) * LANES, LANES), jnp.bfloat16)
    sums = pltpu.VMEM((targets * LANES, LANES), jnp.float32)

    left, *parts = pl.pallas_call(
        functools.partial(near_kernel, columns, code_at),
        in_specs=[smem, vmem, vmem],
        out_specs=[vmem] * (1 + columns),
        out_shape=[left_shape] + [part] * columns,
        scratch_shapes=[pltpu.VMEM((2 * slots * HALF, 2 * LANES), jnp.bfloat16), sums],
        compiler_params=pltpu.CompilerParams(vmem_limit_bytes=16 * MIB + 2 * sums_size),
        cost_estimate=pl.CostEstimate(flops=20_000_000_000, bytes_accessed=8 * MIB, transcendentals=0),
    )(meta, rows_view(own_blocks), rows_view(sibling))

    for number, (straight, crossed) in enumerate(far):
        width = straight.shape[0]
        parts = pl.pallas_call(
            functools.partial(far_kernel, columns, code_at, 1 + number),
            in_specs=[smem] + [vmem] * (3 + columns),
            out_specs=[vmem] * columns,
            out_shape=[part] * columns,
            scratch_shapes=[pltpu.VMEM((2 * width * HALF, 2 * LANES), jnp.bfloat16), sums],
            compiler_params=pltpu.CompilerParams(vmem_limit_bytes=16 * MIB + 2 * sums_size),
            cost_estimate=pl.CostEstimate(flops=8_000_000_000, bytes_accessed=6 * MIB, transcendentals=0),
        )(meta, rows_view(straight), rows_view(crossed), left, *parts)

    arrived = [parts[0]]
    for turn in range(1, columns):
        ahead = [(device, (device + turn) % columns) for device in range(columns)]
        arrived.append(lax.ppermute(parts[turn], "col", ahead))

    owned = pl.pallas_call(
        last_kernel,
        in_specs=[vmem] * columns,
        out_specs=vmem,
        out_shape=jax.ShapeDtypeStruct((SC * HALF, LANES), jnp.float32),
        scratch_shapes=[pltpu.VMEM((LANES, LANES), jnp.float32)],
        compiler_params=pltpu.CompilerParams(vmem_limit_bytes=16 * MIB),
    )(*arrived)
    return blocks_view(owned)[None]


def solution(mesh):
    columns, rows = mesh.shape["col"], mesh.shape["row"]
    return jax.shard_map(
        functools.partial(per_device, columns, rows),
        mesh=mesh,
        in_specs=(P(("groups", "col"), "row", None), P(("groups", "col"), "row", None, None)),
        out_specs=P(("groups", "row"), "col", None),
        check_vma=False,
    )
```

```python
import functools

import jax
import jax.numpy as jnp
from jax import lax
from jax.experimental import pallas as pl
from jax.experimental.pallas import tpu as pltpu
from jax.sharding import PartitionSpec as P

BLK = 64
BB = 4096
SC = 8
HALF = 32
LANES = 128
GROUP = 4
UNROLLS = (32, 8)
HEAD = 256
MIB = 1 << 20


def rows_view(blocks):
    count = blocks.shape[0]
    tiles = blocks.reshape(count // 8, 8, HALF, LANES)
    return tiles.transpose(0, 2, 1, 3).reshape(count * HALF, LANES)


def blocks_view(rows):
    count = rows.shape[0] // HALF
    tiles = rows.reshape(count // 8, HALF, 8, LANES)
    return tiles.transpose(0, 2, 1, 3).reshape(count, BB)


def block_rows(ref, slot):
    start = (slot // 8) * (8 * HALF) + slot % 8
    return ref[pl.ds(start, HALF, stride=8), :]


def high_low(rows):
    high = rows.astype(jnp.bfloat16)
    low = (rows - high.astype(jnp.float32)).astype(jnp.bfloat16)
    return high, low


def fill_right(source, right, first_block, count):
    def one(slot, carry):
        high, low = high_low(block_rows(source, slot))
        at = pl.ds(pl.multiple_of((first_block + slot) * HALF, HALF), HALF)
        right[at, :LANES] = high
        right[at, LANES:] = low
        return carry

    lax.fori_loop(0, count, one, 0, unroll=8)


def fill_left(source, left, count):
    def one(slot, carry):
        high, low = high_low(block_rows(source, slot))
        at = pl.ds(pl.multiple_of(slot * LANES, LANES), LANES)
        left[at, :] = jnp.concatenate([high, low, high, low], axis=0).T
        return carry

    lax.fori_loop(0, count, one, 0, unroll=2)
    left[pl.ds(count * LANES, LANES), :] = jnp.zeros((LANES, LANES), jnp.bfloat16)


def run_groups(meta, bounds, code_at, empty, left, right, sums):
    begin, end = meta[bounds[0]], meta[bounds[1]]
    first_target = bounds[2] * SC
    near = lax.broadcasted_iota(jnp.int32, (LANES, LANES), 1) < BLK

    def multiply(place):
        group = meta[HEAD + place]
        base = group >> 12
        live = jnp.where(place < end, (group >> 8) & 15, 0)
        target = jnp.clip((group & 255) - first_target, 0, sums.shape[0] // LANES - 1)
        lefts, rights = [], []
        for item in range(GROUP):
            code = meta[code_at + base + item]
            own = jnp.where(item < live, code & 63, empty)
            other = jnp.where(item < live, (code >> 6) & 127, 0)
            lefts.append(left[pl.ds(pl.multiple_of(own * LANES, LANES), LANES), :])
            block = right[pl.ds(pl.multiple_of(other * HALF, HALF), HALF), :]
            rights += [block, block]
        stacked = jnp.concatenate(
            [jnp.where(near, lefts[item], lefts[item + 1]) for item in range(0, GROUP, 2)],
            axis=1,
        )
        term = jnp.dot(
            stacked, jnp.concatenate(rights, axis=0), preferred_element_type=jnp.float32
        )
        at = pl.ds(pl.multiple_of(target * LANES, LANES), LANES)
        sums[at, :] += term[:, :LANES] + term[:, LANES:]

    wide, narrow = UNROLLS

    def wide_step(number, carry):
        for inner in range(wide):
            multiply(begin + number * wide + inner)
        return carry

    whole = (end - begin) // wide
    middle = begin + whole * wide

    def narrow_step(number, carry):
        for inner in range(narrow):
            multiply(middle + number * narrow + inner)
        return carry

    lax.fori_loop(0, whole, wide_step, 0)
    lax.fori_loop(0, (end - middle + narrow - 1) // narrow, narrow_step, 0)


def clear(sums):
    def one(number, carry):
        at = pl.ds(pl.multiple_of(number * LANES, LANES), LANES)
        sums[at, :] = jnp.zeros((LANES, LANES), jnp.float32)
        return carry

    lax.fori_loop(0, sums.shape[0] // LANES, one, 0, unroll=2)


def pack_pairs(sums, earlier, outs):
    near = lax.broadcasted_iota(jnp.int32, (BLK, LANES), 1) < BLK
    for place, out in enumerate(outs):
        for pair in range(SC // 2):
            at = (place * SC + 2 * pair) * LANES
            upper0 = sums[at : at + BLK, :]
            lower0 = sums[at + BLK : at + LANES, :]
            upper1 = sums[at + LANES : at + LANES + BLK, :]
            lower1 = sums[at + LANES + BLK : at + 2 * LANES, :]
            one = upper0 + pltpu.roll(lower0, BLK, 1)
            two = pltpu.roll(upper1, BLK, 1) + lower1
            both = jnp.where(near, one, two)
            if earlier:
                both = both + earlier[place][pair]
            out[pair] = both


def product_kernel(code_at, bounds, new_left, sources, earlier, keep, *refs):
    refs = list(refs)
    take = lambda count: [refs.pop(0) for _ in range(count)]
    (meta,) = take(1)
    sources = take(sources)
    left = None if new_left else take(1)[0]
    right = None if sources else take(1)[0]
    earlier = take(earlier)
    left = take(1)[0] if new_left else left
    right = take(1)[0] if keep else right
    sums = refs.pop()
    right = refs.pop() if right is None else right
    if new_left:
        fill_left(sources[0], left, sources[0].shape[0] // HALF)
    at = 0
    for source in sources:
        fill_right(source, right, at, source.shape[0] // HALF)
        at += source.shape[0] // HALF
    clear(sums)
    run_groups(meta, bounds, code_at, left.shape[0] // LANES - 1, left, right, sums)
    pack_pairs(sums, earlier, refs)


def last_kernel(*refs):
    parts, out, turned = refs[:-2], refs[-2], refs[-1]
    for pair in range(SC // 2):
        total = parts[0][pair]
        for part in parts[1:]:
            total = total + part[pair]
        turned[:, :BLK] = total.T
        even = turned[pl.ds(0, BLK, stride=2), :]
        odd = turned[pl.ds(1, BLK, stride=2), :]
        near = lax.broadcasted_iota(jnp.int32, (BLK, LANES), 1) < BLK
        packed = jnp.where(near, even, pltpu.roll(odd, BLK, 1))
        out[pl.ds(2 * pair, HALF, stride=8), :] = packed[:HALF]
        out[pl.ds(2 * pair + 1, HALF, stride=8), :] = packed[HALF:]


def sent_order(columns):
    groups = [list(range(2, columns - 1)), sorted({1, columns - 1} - {0}), [0]]
    return [turns for turns in groups if turns]


def plan(lists, slots, row, col, columns, chips):
    first, second, target = lists[0], lists[1], lists[2]
    entries = first.shape[0]
    targets = columns * SC
    phases = 2 * chips - 1
    shard, slot = first // slots, first % slots
    hop = (shard // 2 - row // 2) % chips
    crossed = (shard ^ row) & 1
    close = hop == 0
    phase = jnp.where(close, 0, 2 * hop - 1 + crossed)
    panel_slot = jnp.where(close, crossed * slots + slot, slot)
    turn = (target // SC - col) % columns
    position = turn
    for number, one in enumerate(sum(sent_order(columns), [])):
        position = jnp.where(turn == one, number, position)
    segments = phases * targets
    segment = jnp.where(target < targets, phase * targets + position * SC + target % SC, segments)
    codes = lax.sort((segment << 13) | (panel_slot << 6) | second)

    edges = jnp.arange(segments + 1)
    sorted_segment = codes >> 13
    starts = jnp.sum((sorted_segment[None, :] < edges[:, None]).astype(jnp.int32), axis=1)
    live = starts[1:] - starts[:-1]
    groups = (live + GROUP - 1) // GROUP
    upto = edges[:-1][None, :] < edges[:, None]
    group_starts = jnp.sum(jnp.where(upto, groups[None, :], 0), axis=1)

    places = -(-(entries // GROUP + segments + UNROLLS[0]) // LANES) * LANES
    place = jnp.arange(places)
    passed = group_starts[1:][None, :] <= place[:, None]
    shift = starts - GROUP * group_starts
    in_segment = jnp.sum(passed.astype(jnp.int32), axis=1)
    offset = shift[0] + jnp.sum(jnp.where(passed, (shift[1:] - shift[:-1])[None, :], 0), axis=1)
    stops = jnp.concatenate([starts[1:], starts[-1:]])
    stop = stops[0] + jnp.sum(jnp.where(passed, (stops[1:] - stops[:-1])[None, :], 0), axis=1)
    base = jnp.clip(GROUP * place + offset, 0, entries)
    valid = jnp.clip(stop - base, 0, GROUP)
    described = (base << 12) | (valid << 8) | (in_segment % targets)

    bounds = group_starts[::SC]
    meta = jnp.concatenate(
        [
            jnp.pad(bounds, (0, HEAD - bounds.shape[0])),
            described,
            codes,
            jnp.zeros((LANES,), jnp.int32),
        ]
    )
    return meta, HEAD + places


def products_of(meta, code_at, columns, phase, places, sources, left, right, earlier, keep=False):
    smem = pl.BlockSpec(memory_space=pltpu.SMEM)
    vmem = pl.BlockSpec(memory_space=pltpu.VMEM)
    part = jax.ShapeDtypeStruct((SC // 2, BLK, LANES), jnp.float32)
    first, last = places
    new_left = left is None
    out_shape = [part] * (last - first)
    slots = sources[0].shape[0] if sources else right.shape[0] // HALF
    right_shape = (max(len(sources), 1) * slots * HALF, 2 * LANES)
    if keep:
        out_shape = [jax.ShapeDtypeStruct(right_shape, jnp.bfloat16)] + out_shape
    if new_left:
        left_shape = ((slots + 1) * LANES, LANES)
        out_shape = [jax.ShapeDtypeStruct(left_shape, jnp.bfloat16)] + out_shape
    scratch = [pltpu.VMEM(((last - first) * SC * LANES, LANES), jnp.float32)]
    if sources and not keep:
        scratch = [pltpu.VMEM(right_shape, jnp.bfloat16)] + scratch
    args = [rows_view(source) for source in sources]
    args += [] if new_left else [left]
    args += [] if sources else [right]
    args += earlier
    bounds = (phase * columns + first, phase * columns + last, first)
    sums_size = (last - first) * SC * LANES * LANES * 4
    return pl.pallas_call(
        functools.partial(
            product_kernel, code_at, bounds, new_left, len(sources), len(earlier), keep
        ),
        in_specs=[smem] + [vmem] * len(args),
        out_specs=[vmem] * len(out_shape),
        out_shape=out_shape,
        scratch_shapes=scratch,
        compiler_params=pltpu.CompilerParams(vmem_limit_bytes=16 * MIB + 2 * sums_size),
        cost_estimate=pl.CostEstimate(flops=1_000_000, bytes_accessed=MIB, transcendentals=0),
    )(meta, *args)


def per_device(columns, rows, p_blocks, products):
    own_blocks = p_blocks[0]
    slots = own_blocks.shape[0]
    chips = rows // 2
    row, col = lax.axis_index("row"), lax.axis_index("col")
    swap = [(device, device ^ 1) for device in range(rows)]

    straight = []
    for hop in range(1, chips):
        jump = [((device + 2 * hop) % rows, device) for device in range(rows)]
        straight.append(lax.ppermute(own_blocks, "row", jump))
    sibling = lax.ppermute(own_blocks, "row", swap)

    meta, code_at = plan(products[0, 0], slots, row, col, columns, chips)
    made = functools.partial(products_of, meta, code_at, columns)
    everything = (0, columns)
    left, *parts = made(0, everything, [own_blocks, sibling], None, None, [])
    for hop, blocks in enumerate(straight):
        blocks, left, *parts = lax.optimization_barrier((blocks, left, *parts))
        crossed = lax.ppermute(blocks, "row", swap)
        parts = made(2 * hop + 1, everything, [blocks], left, None, parts)
        if hop + 1 < len(straight):
            parts = made(2 * hop + 2, everything, [crossed], left, None, parts)

    arrived = []
    begin, right = 0, None
    for turns in sent_order(columns):
        places = (begin, begin + len(turns))
        before = parts[places[0] : places[1]]
        phase = 2 * len(straight)
        if right is None:
            right, *sums = made(phase, places, [crossed], left, None, before, keep=True)
        else:
            sums = made(phase, places, [], left, right, before)
        for turn, part in zip(turns, sums):
            ahead = [(device, (device + turn) % columns) for device in range(columns)]
            arrived.append(lax.ppermute(part, "col", ahead) if turn else part)
        begin = places[1]

    vmem = pl.BlockSpec(memory_space=pltpu.VMEM)
    owned = pl.pallas_call(
        last_kernel,
        in_specs=[vmem] * columns,
        out_specs=vmem,
        out_shape=jax.ShapeDtypeStruct((SC * HALF, LANES), jnp.float32),
        scratch_shapes=[pltpu.VMEM((LANES, LANES), jnp.float32)],
        compiler_params=pltpu.CompilerParams(vmem_limit_bytes=16 * MIB),
    )(*arrived)
    return blocks_view(owned)[None]


def solution(mesh):
    columns, rows = mesh.shape["col"], mesh.shape["row"]
    return jax.shard_map(
        functools.partial(per_device, columns, rows),
        mesh=mesh,
        in_specs=(P(("groups", "col"), "row", None), P(("groups", "col"), "row", None, None)),
        out_specs=P(("groups", "row"), "col", None),
        check_vma=False,
    )
```

```python
import functools

import jax
import jax.numpy as jnp
from jax import lax
from jax.experimental import pallas as pl
from jax.experimental.pallas import tpu as pltpu
from jax.sharding import PartitionSpec as P

BLK = 64
BB = 4096
SC = 8
HALF = 32
LANES = 128
GROUP = 4
UNROLLS = (32, 8)
MIB = 1 << 20


def rows_view(blocks):
    count = blocks.shape[0]
    tiles = blocks.reshape(count // 8, 8, HALF, LANES)
    return tiles.transpose(0, 2, 1, 3).reshape(count * HALF, LANES)


def blocks_view(rows):
    count = rows.shape[0] // HALF
    tiles = rows.reshape(count // 8, HALF, 8, LANES)
    return tiles.transpose(0, 2, 1, 3).reshape(count, BB)


def block_rows(ref, slot):
    start = (slot // 8) * (8 * HALF) + slot % 8
    return ref[pl.ds(start, HALF, stride=8), :]


def high_low(rows):
    high = rows.astype(jnp.bfloat16)
    low = (rows - high.astype(jnp.float32)).astype(jnp.bfloat16)
    return high, low


def fill_right(source, right, first_block, count):
    def one(slot, carry):
        high, low = high_low(block_rows(source, slot))
        at = pl.ds(pl.multiple_of((first_block + slot) * HALF, HALF), HALF)
        right[at, :LANES] = high
        right[at, LANES:] = low
        return carry

    lax.fori_loop(0, count, one, 0, unroll=8)


def fill_left(source, left, count):
    near = lax.broadcasted_iota(jnp.int32, (LANES, LANES), 1) < BLK

    def two(number, carry):
        pair = high_low(block_rows(source, 2 * number)) + high_low(block_rows(source, 2 * number + 1))
        straight = jnp.concatenate(pair, axis=0).T
        turned = pltpu.roll(straight, BLK, 1)
        at = pl.multiple_of(2 * number * LANES, LANES)
        left[pl.ds(at, LANES), :] = jnp.where(near, straight, turned)
        left[pl.ds(at + LANES, LANES), :] = jnp.where(near, turned, straight)
        return carry

    lax.fori_loop(0, count // 2, two, 0, unroll=4)
    left[pl.ds(count * LANES, LANES), :] = jnp.zeros((LANES, LANES), jnp.bfloat16)


def run_groups(meta, layout, bounds, empty, left, right, sums):
    groups_at, code_at = layout
    begin, end = meta[bounds[0]], meta[bounds[1]]
    first_target = bounds[2] * SC
    near = lax.broadcasted_iota(jnp.int32, (LANES, LANES), 1) < BLK

    def multiply(place):
        group = meta[groups_at + place]
        base = group >> 12
        live = jnp.where(place < end, (group >> 8) & 15, 0)
        target = jnp.clip((group & 255) - first_target, 0, sums.shape[0] // LANES - 1)
        lefts, rights = [], []
        for item in range(GROUP):
            code = meta[code_at + base + item]
            own = jnp.where(item < live, code & 63, empty)
            other = jnp.where(item < live, (code >> 6) & 127, 0)
            lefts.append(left[pl.ds(pl.multiple_of(own * LANES, LANES), LANES), :])
            block = right[pl.ds(pl.multiple_of(other * HALF, HALF), HALF), :]
            rights += [block, block]
        stacked = jnp.concatenate(
            [jnp.where(near, lefts[item], lefts[item + 1]) for item in range(0, GROUP, 2)],
            axis=1,
        )
        term = jnp.dot(
            stacked, jnp.concatenate(rights, axis=0), preferred_element_type=jnp.float32
        )
        at = pl.ds(pl.multiple_of(target * LANES, LANES), LANES)
        sums[at, :] += term[:, :LANES] + term[:, LANES:]

    wide, narrow = UNROLLS

    def wide_step(number, carry):
        for inner in range(wide):
            multiply(begin + number * wide + inner)
        return carry

    whole = (end - begin) // wide
    middle = begin + whole * wide

    def narrow_step(number, carry):
        for inner in range(narrow):
            multiply(middle + number * narrow + inner)
        return carry

    lax.fori_loop(0, whole, wide_step, 0)
    lax.fori_loop(0, (end - middle + narrow - 1) // narrow, narrow_step, 0)


def clear(sums):
    def one(number, carry):
        at = pl.ds(pl.multiple_of(number * LANES, LANES), LANES)
        sums[at, :] = jnp.zeros((LANES, LANES), jnp.float32)
        return carry

    lax.fori_loop(0, sums.shape[0] // LANES, one, 0, unroll=2)


def pack_pairs(sums, earlier, outs):
    near = lax.broadcasted_iota(jnp.int32, (BLK, LANES), 1) < BLK
    for place, out in enumerate(outs):
        for pair in range(SC // 2):
            at = (place * SC + 2 * pair) * LANES
            upper0 = sums[at : at + BLK, :]
            lower0 = sums[at + BLK : at + LANES, :]
            upper1 = sums[at + LANES : at + LANES + BLK, :]
            lower1 = sums[at + LANES + BLK : at + 2 * LANES, :]
            turned = pltpu.roll(jnp.where(near, upper1, lower0), BLK, 1)
            both = jnp.where(near, upper0, lower1) + turned
            for part in earlier[place :: len(outs)]:
                both = both + part[pair]
            out[pair] = both


def product_kernel(layout, bounds, new_left, rights, keep, earlier, meta, left, *refs):
    refs, sums = list(refs[:-1]), refs[-1]
    sources, earlier, refs = refs[:rights], refs[rights : rights + earlier], refs[rights + earlier :]
    if new_left:
        source, left = left, refs.pop(0)
        fill_left(source, left, source.shape[0] // HALF)
    if any(source.dtype == jnp.float32 for source in sources):
        right, at = refs.pop(0) if keep else refs.pop(), 0
        for source in sources:
            rows = source.shape[0]
            if source.dtype == jnp.float32:
                fill_right(source, right, at // HALF, rows // HALF)
            else:
                right[at : at + rows, :] = source[...]
            at += rows
    else:
        (right,) = sources
    clear(sums)
    run_groups(meta, layout, bounds, left.shape[0] // LANES - 1, left, right, sums)
    pack_pairs(sums, earlier, refs)


def last_kernel(*refs):
    parts, out, turned = refs[:-2], refs[-2], refs[-1]
    for pair in range(SC // 2):
        total = parts[0][pair]
        for part in parts[1:]:
            total = total + part[pair]
        turned[:, :BLK] = total.T
        even = turned[pl.ds(0, BLK, stride=2), :]
        odd = turned[pl.ds(1, BLK, stride=2), :]
        near = lax.broadcasted_iota(jnp.int32, (BLK, LANES), 1) < BLK
        packed = jnp.where(near, even, pltpu.roll(odd, BLK, 1))
        out[pl.ds(2 * pair, HALF, stride=8), :] = packed[:HALF]
        out[pl.ds(2 * pair + 1, HALF, stride=8), :] = packed[HALF:]


def sent_order(columns):
    half = columns // 2
    cut = half + half // 2
    groups = [range(half, cut), range(cut, columns), range(1, half), range(1)]
    return [list(pairs) for pairs in groups if len(pairs)]


def plan(lists, slots, row, col, columns, chips):
    first, second, target = lists[0], lists[1], lists[2]
    entries = first.shape[0]
    targets = columns * SC
    phases = chips + 1
    shard, slot = first // slots, first % slots
    hop = (shard // 2 - row // 2) % chips
    crossed = (shard ^ row) & 1
    pair = (target // SC) ^ col
    half = columns // 2
    position = jnp.where(pair >= half, pair - half, jnp.where(pair == 0, columns, pair + half) - 1)
    apart = (hop == chips - 1) & (position < len(sent_order(columns)[0]))
    phase = hop + jnp.where(apart, crossed, 0)
    slot = crossed * slots + slot
    segments = phases * targets
    segment = jnp.where(target < targets, phase * targets + position * SC + target % SC, segments)
    (codes,) = lax.sort(((segment << 13) | (slot << 6) | second,), is_stable=False)

    count = lambda chosen, amount: jnp.sum(jnp.where(chosen, amount, 0), axis=1)
    edges = jnp.arange(segments)
    live = count((codes >> 13)[None, :] == edges[:, None], 1)
    groups = (live + GROUP - 1) // GROUP
    stops = count(edges[None, :] <= edges[:, None], groups[None, :])
    places = -(-(entries // GROUP + segments + UNROLLS[0]) // LANES) * LANES
    place = jnp.arange(places)[:, None]
    passed = stops[None, :] <= place
    in_segment = count(passed, 1)
    base = GROUP * place[:, 0] + count(passed, (live - GROUP * groups)[None, :])
    base = jnp.clip(base, 0, entries)
    stop = count((stops - groups)[None, :] <= place, live[None, :])
    valid = jnp.clip(stop - base, 0, GROUP)
    described = (base << 12) | (valid << 8) | (in_segment % targets)

    head = -(-(segments // SC + 1) // LANES) * LANES
    bounds = count(edges[None, :] < SC * jnp.arange(head)[:, None], groups[None, :])
    meta = jnp.concatenate([bounds, described, codes, jnp.zeros((LANES,), jnp.int32)])
    return meta, (head, head + places)


def products_of(columns, meta, layout, phase, places, left, rights, earlier, keep=False):
    smem = pl.BlockSpec(memory_space=pltpu.SMEM)
    vmem = pl.BlockSpec(memory_space=pltpu.VMEM)
    part = jax.ShapeDtypeStruct((SC // 2, BLK, LANES), jnp.float32)
    first, last = places
    targets = (last - first) * SC
    out_shape, scratch = [], [pltpu.VMEM((targets * LANES, LANES), jnp.float32)]
    new_left = left.dtype == jnp.float32
    if new_left:
        out_shape.append(jax.ShapeDtypeStruct(((left.shape[0] + 1) * LANES, LANES), jnp.bfloat16))
        left = rows_view(left)
    new_right = any(right.dtype == jnp.float32 for right in rights)
    rights = [rows_view(right) if right.dtype == jnp.float32 else right for right in rights]
    if new_right:
        table = (sum(right.shape[0] for right in rights), 2 * LANES)
        if keep:
            out_shape.append(jax.ShapeDtypeStruct(table, jnp.bfloat16))
        else:
            scratch.insert(0, pltpu.VMEM(table, jnp.bfloat16))
    out_shape += [part] * (last - first)
    bounds = (phase * columns + first, phase * columns + last, first)
    args = [left, *rights, *earlier]
    return pl.pallas_call(
        functools.partial(
            product_kernel, layout, bounds, new_left, len(rights), keep, len(earlier)
        ),
        in_specs=[smem] + [vmem] * len(args),
        out_specs=[vmem] * len(out_shape),
        out_shape=out_shape,
        scratch_shapes=scratch,
        compiler_params=pltpu.CompilerParams(
            vmem_limit_bytes=16 * MIB + 8 * targets * LANES * LANES
        ),
        cost_estimate=pl.CostEstimate(flops=1_000_000, bytes_accessed=MIB, transcendentals=0),
    )(meta, *args)


def per_device(columns, rows, p_blocks, products):
    own_blocks = p_blocks[0]
    slots = own_blocks.shape[0]
    chips = rows // 2
    row, col = lax.axis_index("row"), lax.axis_index("col")
    swap = [(device, device ^ 1) for device in range(rows)]

    arriving = []
    for hop in range(1, chips):
        jump = [((device + 2 * hop) % rows, device) for device in range(rows)]
        arriving.append(lax.ppermute(own_blocks, "row", jump))
    sibling_blocks = lax.ppermute(own_blocks, "row", swap)

    made = functools.partial(
        products_of, columns, *plan(products[0, 0], slots, row, col, columns, chips)
    )
    whole = (0, columns)
    left, *parts = made(0, whole, own_blocks, [own_blocks, sibling_blocks], [])
    for hop, blocks in enumerate(arriving[:-1], 1):
        blocks, left, *parts = lax.optimization_barrier((blocks, left, *parts))
        parts = made(hop, whole, left, [blocks, lax.ppermute(blocks, "row", swap)], parts)
    blocks, left, *parts = lax.optimization_barrier((arriving[-1], left, *parts))
    crossed = lax.ppermute(blocks, "row", swap)

    arrived, early, begin = [], [], 0
    for number, pairs in enumerate(sent_order(columns)):
        end = begin + len(pairs)
        places, earlier = (begin, end), parts[begin:end]
        if number == 0:
            right, *earlier = made(chips - 1, places, left, [blocks], earlier, keep=True)
            right, *sums = made(chips, places, left, [right, crossed], earlier, keep=True)
        else:
            if pairs == [0]:
                earlier = [*earlier, *early]
            sums = made(chips - 1, places, left, [right], earlier)
        for pair, part in zip(pairs, sums):
            across = [(device, device ^ pair) for device in range(columns)]
            moved = lax.ppermute(part, "col", across) if pair else part
            (arrived if number else early).append(moved)
        begin = end

    vmem = pl.BlockSpec(memory_space=pltpu.VMEM)
    owned = pl.pallas_call(
        last_kernel,
        in_specs=[vmem] * len(arrived),
        out_specs=vmem,
        out_shape=jax.ShapeDtypeStruct((SC * HALF, LANES), jnp.float32),
        scratch_shapes=[pltpu.VMEM((LANES, LANES), jnp.float32)],
        compiler_params=pltpu.CompilerParams(vmem_limit_bytes=16 * MIB),
    )(*arrived)
    return blocks_view(owned)[None]


def solution(mesh):
    columns, rows = mesh.shape["col"], mesh.shape["row"]
    return jax.shard_map(
        functools.partial(per_device, columns, rows),
        mesh=mesh,
        in_specs=(P(("groups", "col"), "row", None), P(("groups", "col"), "row", None, None)),
        out_specs=P(("groups", "row"), "col", None),
        check_vma=False,
    )
```

```python
import functools

import jax
import jax.numpy as jnp
from jax import lax
from jax.experimental import pallas as pl
from jax.experimental.pallas import tpu as pltpu
from jax.sharding import PartitionSpec as P

BLK = 64
BB = 4096
SC = 8
HALF = 32
LANES = 128
GROUP = 4
UNROLLS = (32, 8)
MIB = 1 << 20


def rows_view(blocks):
    count = blocks.shape[0]
    tiles = blocks.reshape(count // 8, 8, HALF, LANES)
    return tiles.transpose(0, 2, 1, 3).reshape(count * HALF, LANES)


def blocks_view(rows):
    count = rows.shape[0] // HALF
    tiles = rows.reshape(count // 8, HALF, 8, LANES)
    return tiles.transpose(0, 2, 1, 3).reshape(count, BB)


def block_rows(ref, slot):
    start = (slot // 8) * (8 * HALF) + slot % 8
    return ref[pl.ds(start, HALF, stride=8), :]


def high_low(rows):
    high = rows.astype(jnp.bfloat16)
    low = (rows - high.astype(jnp.float32)).astype(jnp.bfloat16)
    return high, low


def fill_right(source, right, first_block, count):
    def one(slot, carry):
        high, low = high_low(block_rows(source, slot))
        at = pl.ds(pl.multiple_of((first_block + slot) * HALF, HALF), HALF)
        right[at, :LANES] = high
        right[at, LANES:] = low
        return carry

    lax.fori_loop(0, count, one, 0, unroll=8)


def fill_left(source, left, count):
    near = lax.broadcasted_iota(jnp.int32, (LANES, LANES), 1) < BLK

    def two(number, carry):
        pair = high_low(block_rows(source, 2 * number)) + high_low(block_rows(source, 2 * number + 1))
        straight = jnp.concatenate(pair, axis=0).T
        turned = pltpu.roll(straight, BLK, 1)
        at = pl.multiple_of(2 * number * LANES, LANES)
        left[pl.ds(at, LANES), :] = jnp.where(near, straight, turned)
        left[pl.ds(at + LANES, LANES), :] = jnp.where(near, turned, straight)
        return carry

    lax.fori_loop(0, count // 2, two, 0, unroll=4)
    left[pl.ds(count * LANES, LANES), :] = jnp.zeros((LANES, LANES), jnp.bfloat16)


def run_groups(meta, layout, bounds, empty, left, right, sums):
    groups_at, code_at = layout
    begin, end = meta[bounds[0]], meta[bounds[1]]
    first_target = bounds[2] * SC
    near = lax.broadcasted_iota(jnp.int32, (LANES, LANES), 1) < BLK

    def multiply(place):
        group = meta[groups_at + place]
        base = group >> 12
        live = jnp.where(place < end, (group >> 8) & 15, 0)
        target = jnp.clip((group & 255) - first_target, 0, sums.shape[0] // LANES - 1)
        lefts, rights = [], []
        for item in range(GROUP):
            code = meta[code_at + base + item]
            own = jnp.where(item < live, code & 63, empty)
            other = jnp.where(item < live, (code >> 6) & 127, 0)
            lefts.append(left[pl.ds(pl.multiple_of(own * LANES, LANES), LANES), :])
            block = right[pl.ds(pl.multiple_of(other * HALF, HALF), HALF), :]
            rights += [block, block]
        stacked = jnp.concatenate(
            [jnp.where(near, lefts[item], lefts[item + 1]) for item in range(0, GROUP, 2)],
            axis=1,
        )
        term = jnp.dot(
            stacked, jnp.concatenate(rights, axis=0), preferred_element_type=jnp.float32
        )
        at = pl.ds(pl.multiple_of(target * LANES, LANES), LANES)
        sums[at, :] += term[:, :LANES] + term[:, LANES:]

    wide, narrow = UNROLLS

    def wide_step(number, carry):
        for inner in range(wide):
            multiply(begin + number * wide + inner)
        return carry

    whole = (end - begin) // wide
    middle = begin + whole * wide

    def narrow_step(number, carry):
        for inner in range(narrow):
            multiply(middle + number * narrow + inner)
        return carry

    lax.fori_loop(0, whole, wide_step, 0)
    lax.fori_loop(0, (end - middle + narrow - 1) // narrow, narrow_step, 0)


def clear(sums):
    def one(number, carry):
        at = pl.ds(pl.multiple_of(number * LANES, LANES), LANES)
        sums[at, :] = jnp.zeros((LANES, LANES), jnp.float32)
        return carry

    lax.fori_loop(0, sums.shape[0] // LANES, one, 0, unroll=2)


def pack_pairs(sums, earlier, outs):
    near = lax.broadcasted_iota(jnp.int32, (BLK, LANES), 1) < BLK
    for place, out in enumerate(outs):
        for pair in range(SC // 2):
            at = (place * SC + 2 * pair) * LANES
            upper0 = sums[at : at + BLK, :]
            lower0 = sums[at + BLK : at + LANES, :]
            upper1 = sums[at + LANES : at + LANES + BLK, :]
            lower1 = sums[at + LANES + BLK : at + 2 * LANES, :]
            turned = pltpu.roll(jnp.where(near, upper1, lower0), BLK, 1)
            both = jnp.where(near, upper0, lower1) + turned
            for part in earlier[place :: len(outs)]:
                both = both + part[pair]
            out[pair] = both


def product_kernel(layout, bounds, new_left, rights, keep, earlier, meta, left, *refs):
    refs, sums = list(refs[:-1]), refs[-1]
    sources, earlier, refs = refs[:rights], refs[rights : rights + earlier], refs[rights + earlier :]
    if new_left:
        source, left = left, refs.pop(0)
        fill_left(source, left, source.shape[0] // HALF)
    if any(source.dtype == jnp.float32 for source in sources):
        right, at = refs.pop(0) if keep else refs.pop(), 0
        for source in sources:
            rows = source.shape[0]
            if source.dtype == jnp.float32:
                fill_right(source, right, at // HALF, rows // HALF)
            else:
                right[at : at + rows, :] = source[...]
            at += rows
    else:
        (right,) = sources
    clear(sums)
    run_groups(meta, layout, bounds, left.shape[0] // LANES - 1, left, right, sums)
    pack_pairs(sums, earlier, refs)


def last_kernel(*refs):
    parts, out, turned = refs[:-2], refs[-2], refs[-1]
    for pair in range(SC // 2):
        total = parts[0][pair]
        for part in parts[1:]:
            total = total + part[pair]
        turned[:, :BLK] = total.T
        even = turned[pl.ds(0, BLK, stride=2), :]
        odd = turned[pl.ds(1, BLK, stride=2), :]
        near = lax.broadcasted_iota(jnp.int32, (BLK, LANES), 1) < BLK
        packed = jnp.where(near, even, pltpu.roll(odd, BLK, 1))
        out[pl.ds(2 * pair, HALF, stride=8), :] = packed[:HALF]
        out[pl.ds(2 * pair + 1, HALF, stride=8), :] = packed[HALF:]


def sent_order(columns):
    half = columns // 2
    cut = half + half // 2
    groups = [range(half, cut), range(cut, columns), range(1, half), range(1)]
    return [list(pairs) for pairs in groups if len(pairs)]


def plan(lists, slots, row, col, columns, chips):
    first, second, target = lists[0], lists[1], lists[2]
    entries = first.shape[0]
    targets = columns * SC
    phases = chips + 1
    shard, slot = first // slots, first % slots
    hop = (shard // 2 - row // 2) % chips
    crossed = (shard ^ row) & 1
    pair = (target // SC) ^ col
    half = columns // 2
    position = jnp.where(pair >= half, pair - half, jnp.where(pair == 0, columns, pair + half) - 1)
    apart = (hop == chips - 1) & (position < len(sent_order(columns)[0]))
    phase = hop + jnp.where(apart, crossed, 0)
    slot = crossed * slots + slot
    segments = phases * targets
    segment = jnp.where(target < targets, phase * targets + position * SC + target % SC, segments)
    (codes,) = lax.sort(((segment << 13) | (slot << 6) | second,), is_stable=False)

    count = lambda chosen, amount: jnp.sum(jnp.where(chosen, amount, 0), axis=1)
    edges = jnp.arange(segments)
    live = count((codes >> 13)[None, :] == edges[:, None], 1)
    groups = (live + GROUP - 1) // GROUP
    stops = count(edges[None, :] <= edges[:, None], groups[None, :])
    places = -(-(entries // GROUP + segments + UNROLLS[0]) // LANES) * LANES
    place = jnp.arange(places)[:, None]
    passed = stops[None, :] <= place
    in_segment = count(passed, 1)
    base = GROUP * place[:, 0] + count(passed, (live - GROUP * groups)[None, :])
    base = jnp.clip(base, 0, entries)
    stop = count((stops - groups)[None, :] <= place, live[None, :])
    valid = jnp.clip(stop - base, 0, GROUP)
    described = (base << 12) | (valid << 8) | (in_segment % targets)

    head = -(-(segments // SC + 1) // LANES) * LANES
    bounds = count(edges[None, :] < SC * jnp.arange(head)[:, None], groups[None, :])
    meta = jnp.concatenate([bounds, described, codes, jnp.zeros((LANES,), jnp.int32)])
    return meta, (head, head + places)


def products_of(
    columns, meta, layout, phase, places, left, rights, earlier, keep=False, work=1_000_000
):
    smem = pl.BlockSpec(memory_space=pltpu.SMEM)
    vmem = pl.BlockSpec(memory_space=pltpu.VMEM)
    part = jax.ShapeDtypeStruct((SC // 2, BLK, LANES), jnp.float32)
    first, last = places
    targets = (last - first) * SC
    out_shape, scratch = [], [pltpu.VMEM((targets * LANES, LANES), jnp.float32)]
    new_left = left.dtype == jnp.float32
    if new_left:
        out_shape.append(jax.ShapeDtypeStruct(((left.shape[0] + 1) * LANES, LANES), jnp.bfloat16))
        left = rows_view(left)
    new_right = any(right.dtype == jnp.float32 for right in rights)
    rights = [rows_view(right) if right.dtype == jnp.float32 else right for right in rights]
    if new_right:
        table = (sum(right.shape[0] for right in rights), 2 * LANES)
        if keep:
            out_shape.append(jax.ShapeDtypeStruct(table, jnp.bfloat16))
        else:
            scratch.insert(0, pltpu.VMEM(table, jnp.bfloat16))
    out_shape += [part] * (last - first)
    bounds = (phase * columns + first, phase * columns + last, first)
    args = [left, *rights, *earlier]
    return pl.pallas_call(
        functools.partial(
            product_kernel, layout, bounds, new_left, len(rights), keep, len(earlier)
        ),
        in_specs=[smem] + [vmem] * len(args),
        out_specs=[vmem] * len(out_shape),
        out_shape=out_shape,
        scratch_shapes=scratch,
        compiler_params=pltpu.CompilerParams(
            vmem_limit_bytes=16 * MIB + 8 * targets * LANES * LANES
        ),
        cost_estimate=pl.CostEstimate(flops=work, bytes_accessed=MIB, transcendentals=0),
    )(meta, *args)


def per_device(columns, rows, p_blocks, products):
    own_blocks = p_blocks[0]
    slots = own_blocks.shape[0]
    chips = rows // 2
    row, col = lax.axis_index("row"), lax.axis_index("col")
    swap = [(device, device ^ 1) for device in range(rows)]

    arriving = []
    for hop in range(1, chips):
        jump = [((device + 2 * hop) % rows, device) for device in range(rows)]
        arriving.append(lax.ppermute(own_blocks, "row", jump))
    lists, own_again = lax.optimization_barrier((products[0, 0], own_blocks))
    sibling_blocks = lax.ppermute(own_again, "row", swap)

    made = functools.partial(
        products_of, columns, *plan(lists, slots, row, col, columns, chips)
    )
    whole = (0, columns)
    left, *parts = made(0, whole, own_blocks, [own_blocks, sibling_blocks], [])
    for hop, blocks in enumerate(arriving[:-1], 1):
        blocks, left, *parts = lax.optimization_barrier((blocks, left, *parts))
        parts = made(hop, whole, left, [blocks, lax.ppermute(blocks, "row", swap)], parts)
    blocks, left, *parts = lax.optimization_barrier((arriving[-1], left, *parts))
    crossed = lax.ppermute(blocks, "row", swap)

    arrived, early, begin, sums = [], [], 0, []
    for number, pairs in enumerate(sent_order(columns)):
        end = begin + len(pairs)
        sums, parts = lax.optimization_barrier((sums, parts))
        places, earlier = (begin, end), parts[begin:end]
        if number == 0:
            right, *earlier = made(chips - 1, places, left, [blocks], earlier, keep=True)
            right, *sums = made(chips, places, left, [right, crossed], earlier, keep=True)
        else:
            if pairs == [0]:
                earlier = [*earlier, *early]
            work = 5_000_000_000 if pairs == [0] else 1_000_000
            sums = made(chips - 1, places, left, [right], earlier, work=work)
        for pair, part in zip(pairs, sums):
            across = [(device, device ^ pair) for device in range(columns)]
            moved = lax.ppermute(part, "col", across) if pair else part
            (arrived if number else early).append(moved)
        begin = end

    vmem = pl.BlockSpec(memory_space=pltpu.VMEM)
    owned = pl.pallas_call(
        last_kernel,
        in_specs=[vmem] * len(arrived),
        out_specs=vmem,
        out_shape=jax.ShapeDtypeStruct((SC * HALF, LANES), jnp.float32),
        scratch_shapes=[pltpu.VMEM((LANES, LANES), jnp.float32)],
        compiler_params=pltpu.CompilerParams(vmem_limit_bytes=16 * MIB),
    )(*arrived)
    return blocks_view(owned)[None]


def solution(mesh):
    columns, rows = mesh.shape["col"], mesh.shape["row"]
    return jax.shard_map(
        functools.partial(per_device, columns, rows),
        mesh=mesh,
        in_specs=(P(("groups", "col"), "row", None), P(("groups", "col"), "row", None, None)),
        out_specs=P(("groups", "row"), "col", None),
        check_vma=False,
    )
```

```python
import functools

import jax
import jax.numpy as jnp
from jax import lax
from jax.experimental import pallas as pl
from jax.experimental.pallas import tpu as pltpu
from jax.sharding import PartitionSpec as P

BLK = 64
BB = 4096
SC = 8
HALF = 32
LANES = 128
GROUP = 4
UNROLLS = (32, 8)
MIB = 1 << 20


def rows_view(blocks):
    count = blocks.shape[0]
    tiles = blocks.reshape(count // 8, 8, HALF, LANES)
    return tiles.transpose(0, 2, 1, 3).reshape(count * HALF, LANES)


def blocks_view(rows):
    count = rows.shape[0] // HALF
    tiles = rows.reshape(count // 8, HALF, 8, LANES)
    return tiles.transpose(0, 2, 1, 3).reshape(count, BB)


def block_rows(ref, slot):
    start = (slot // 8) * (8 * HALF) + slot % 8
    return ref[pl.ds(start, HALF, stride=8), :]


def high_low(rows):
    high = rows.astype(jnp.bfloat16)
    low = (rows - high.astype(jnp.float32)).astype(jnp.bfloat16)
    return high, low


def fill_right(source, right, first_block, count):
    def one(slot, carry):
        high, low = high_low(block_rows(source, slot))
        at = pl.ds(pl.multiple_of((first_block + slot) * HALF, HALF), HALF)
        right[at, :LANES] = high
        right[at, LANES:] = low
        return carry

    lax.fori_loop(0, count, one, 0, unroll=8)


def fill_left(source, left, count):
    near = lax.broadcasted_iota(jnp.int32, (LANES, LANES), 1) < BLK

    def two(number, carry):
        pair = high_low(block_rows(source, 2 * number)) + high_low(block_rows(source, 2 * number + 1))
        straight = jnp.concatenate(pair, axis=0).T
        turned = pltpu.roll(straight, BLK, 1)
        at = pl.multiple_of(2 * number * LANES, LANES)
        left[pl.ds(at, LANES), :] = jnp.where(near, straight, turned)
        left[pl.ds(at + LANES, LANES), :] = jnp.where(near, turned, straight)
        return carry

    lax.fori_loop(0, count // 2, two, 0, unroll=4)
    left[pl.ds(count * LANES, LANES), :] = jnp.zeros((LANES, LANES), jnp.bfloat16)


def run_groups(meta, layout, bounds, empty, left, right, sums):
    groups_at, code_at = layout
    begin, end = meta[bounds[0]], meta[bounds[1]]
    first_target = bounds[2] * SC
    near = lax.broadcasted_iota(jnp.int32, (LANES, LANES), 1) < BLK

    def multiply(place):
        group = meta[groups_at + place]
        base = group >> 12
        live = jnp.where(place < end, (group >> 8) & 15, 0)
        target = jnp.clip((group & 255) - first_target, 0, sums.shape[0] // LANES - 1)
        lefts, rights = [], []
        for item in range(GROUP):
            code = meta[code_at + base + item]
            own = jnp.where(item < live, code & 63, empty)
            other = jnp.where(item < live, (code >> 6) & 127, 0)
            lefts.append(left[pl.ds(pl.multiple_of(own * LANES, LANES), LANES), :])
            block = right[pl.ds(pl.multiple_of(other * HALF, HALF), HALF), :]
            rights += [block, block]
        stacked = jnp.concatenate(
            [jnp.where(near, lefts[item], lefts[item + 1]) for item in range(0, GROUP, 2)],
            axis=1,
        )
        term = jnp.dot(
            stacked, jnp.concatenate(rights, axis=0), preferred_element_type=jnp.float32
        )
        at = pl.ds(pl.multiple_of(target * LANES, LANES), LANES)
        sums[at, :] += term[:, :LANES] + term[:, LANES:]

    wide, narrow = UNROLLS

    def wide_step(number, carry):
        for inner in range(wide):
            multiply(begin + number * wide + inner)
        return carry

    whole = (end - begin) // wide
    middle = begin + whole * wide

    def narrow_step(number, carry):
        for inner in range(narrow):
            multiply(middle + number * narrow + inner)
        return carry

    lax.fori_loop(0, whole, wide_step, 0)
    lax.fori_loop(0, (end - middle + narrow - 1) // narrow, narrow_step, 0)


def clear(sums):
    def one(number, carry):
        at = pl.ds(pl.multiple_of(number * LANES, LANES), LANES)
        sums[at, :] = jnp.zeros((LANES, LANES), jnp.float32)
        return carry

    lax.fori_loop(0, sums.shape[0] // LANES, one, 0, unroll=2)


def pack_pairs(sums, earlier, outs):
    near = lax.broadcasted_iota(jnp.int32, (BLK, LANES), 1) < BLK
    for place, out in enumerate(outs):
        for pair in range(SC // 2):
            at = (place * SC + 2 * pair) * LANES
            upper0 = sums[at : at + BLK, :]
            lower0 = sums[at + BLK : at + LANES, :]
            upper1 = sums[at + LANES : at + LANES + BLK, :]
            lower1 = sums[at + LANES + BLK : at + 2 * LANES, :]
            turned = pltpu.roll(jnp.where(near, upper1, lower0), BLK, 1)
            both = jnp.where(near, upper0, lower1) + turned
            for part in earlier[place :: len(outs)]:
                both = both + part[pair]
            out[pair] = both


def product_kernel(layout, bounds, new_left, rights, keep, earlier, meta, left, *refs):
    refs, sums = list(refs[:-1]), refs[-1]
    sources, earlier, refs = refs[:rights], refs[rights : rights + earlier], refs[rights + earlier :]
    if new_left:
        source, left = left, refs.pop(0)
        fill_left(source, left, source.shape[0] // HALF)
    if any(source.dtype == jnp.float32 for source in sources):
        right, at = refs.pop(0) if keep else refs.pop(), 0
        for source in sources:
            rows = source.shape[0]
            if source.dtype == jnp.float32:
                fill_right(source, right, at // HALF, rows // HALF)
            else:
                right[at : at + rows, :] = source[...]
            at += rows
    else:
        (right,) = sources
    clear(sums)
    run_groups(meta, layout, bounds, left.shape[0] // LANES - 1, left, right, sums)
    pack_pairs(sums, earlier, refs)


def last_kernel(*refs):
    parts, out, turned = refs[:-2], refs[-2], refs[-1]
    for pair in range(SC // 2):
        total = parts[0][pair]
        for part in parts[1:]:
            total = total + part[pair]
        turned[:, :BLK] = total.T
        even = turned[pl.ds(0, BLK, stride=2), :]
        odd = turned[pl.ds(1, BLK, stride=2), :]
        near = lax.broadcasted_iota(jnp.int32, (BLK, LANES), 1) < BLK
        packed = jnp.where(near, even, pltpu.roll(odd, BLK, 1))
        out[pl.ds(2 * pair, HALF, stride=8), :] = packed[:HALF]
        out[pl.ds(2 * pair + 1, HALF, stride=8), :] = packed[HALF:]


def sent_order(columns):
    half = columns // 2
    cut = half + half // 2
    groups = [range(half, cut), [*range(cut, columns), *range(1, half)], range(1)]
    return [list(pairs) for pairs in groups if len(pairs)]


def plan(lists, slots, row, col, columns, chips):
    first, second, target = lists[0], lists[1], lists[2]
    entries = first.shape[0]
    targets = columns * SC
    phases = chips + 1
    shard, slot = first // slots, first % slots
    hop = (shard // 2 - row // 2) % chips
    crossed = (shard ^ row) & 1
    pair = (target // SC) ^ col
    half = columns // 2
    position = jnp.where(pair >= half, pair - half, jnp.where(pair == 0, columns, pair + half) - 1)
    apart = (hop == chips - 1) & (position < len(sent_order(columns)[0]))
    phase = hop + jnp.where(apart, crossed, 0)
    slot = crossed * slots + slot
    segments = phases * targets
    segment = jnp.where(target < targets, phase * targets + position * SC + target % SC, segments)
    (codes,) = lax.sort(((segment << 13) | (slot << 6) | second,), is_stable=False)

    count = lambda chosen, amount: jnp.sum(jnp.where(chosen, amount, 0), axis=1)
    edges = jnp.arange(segments)
    live = count((codes >> 13)[None, :] == edges[:, None], 1)
    groups = (live + GROUP - 1) // GROUP
    stops = count(edges[None, :] <= edges[:, None], groups[None, :])
    places = -(-(entries // GROUP + segments + UNROLLS[0]) // LANES) * LANES
    place = jnp.arange(places)[:, None]
    passed = stops[None, :] <= place
    in_segment = count(passed, 1)
    base = GROUP * place[:, 0] + count(passed, (live - GROUP * groups)[None, :])
    base = jnp.clip(base, 0, entries)
    stop = count((stops - groups)[None, :] <= place, live[None, :])
    valid = jnp.clip(stop - base, 0, GROUP)
    described = (base << 12) | (valid << 8) | (in_segment % targets)

    head = -(-(segments // SC + 1) // LANES) * LANES
    bounds = count(edges[None, :] < SC * jnp.arange(head)[:, None], groups[None, :])
    meta = jnp.concatenate([bounds, described, codes, jnp.zeros((LANES,), jnp.int32)])
    return meta, (head, head + places)


def products_of(
    columns, meta, layout, phase, places, left, rights, earlier, keep=False, work=1_000_000
):
    smem = pl.BlockSpec(memory_space=pltpu.SMEM)
    vmem = pl.BlockSpec(memory_space=pltpu.VMEM)
    part = jax.ShapeDtypeStruct((SC // 2, BLK, LANES), jnp.float32)
    first, last = places
    targets = (last - first) * SC
    out_shape, scratch = [], [pltpu.VMEM((targets * LANES, LANES), jnp.float32)]
    new_left = left.dtype == jnp.float32
    if new_left:
        out_shape.append(jax.ShapeDtypeStruct(((left.shape[0] + 1) * LANES, LANES), jnp.bfloat16))
        left = rows_view(left)
    new_right = any(right.dtype == jnp.float32 for right in rights)
    rights = [rows_view(right) if right.dtype == jnp.float32 else right for right in rights]
    if new_right:
        table = (sum(right.shape[0] for right in rights), 2 * LANES)
        if keep:
            out_shape.append(jax.ShapeDtypeStruct(table, jnp.bfloat16))
        else:
            scratch.insert(0, pltpu.VMEM(table, jnp.bfloat16))
    out_shape += [part] * (last - first)
    bounds = (phase * columns + first, phase * columns + last, first)
    args = [left, *rights, *earlier]
    return pl.pallas_call(
        functools.partial(
            product_kernel, layout, bounds, new_left, len(rights), keep, len(earlier)
        ),
        in_specs=[smem] + [vmem] * len(args),
        out_specs=[vmem] * len(out_shape),
        out_shape=out_shape,
        scratch_shapes=scratch,
        compiler_params=pltpu.CompilerParams(
            vmem_limit_bytes=16 * MIB + 8 * targets * LANES * LANES
        ),
        cost_estimate=pl.CostEstimate(flops=work, bytes_accessed=MIB, transcendentals=0),
    )(meta, *args)


def per_device(columns, rows, p_blocks, products):
    own_blocks = p_blocks[0]
    slots = own_blocks.shape[0]
    chips = rows // 2
    row, col = lax.axis_index("row"), lax.axis_index("col")
    swap = [(device, device ^ 1) for device in range(rows)]

    arriving = []
    for hop in range(1, chips):
        jump = [((device + 2 * hop) % rows, device) for device in range(rows)]
        arriving.append(lax.ppermute(own_blocks, "row", jump))
    lists, own_again = lax.optimization_barrier((products[0, 0], own_blocks))
    sibling_blocks = lax.ppermute(own_again, "row", swap)

    made = functools.partial(
        products_of, columns, *plan(lists, slots, row, col, columns, chips)
    )
    whole = (0, columns)
    left, *parts = made(0, whole, own_blocks, [own_blocks, sibling_blocks], [])
    for hop, blocks in enumerate(arriving[:-1], 1):
        blocks, left, *parts = lax.optimization_barrier((blocks, left, *parts))
        parts = made(hop, whole, left, [blocks, lax.ppermute(blocks, "row", swap)], parts)
    blocks, left, *parts = lax.optimization_barrier((arriving[-1], left, *parts))
    crossed = lax.ppermute(blocks, "row", swap)

    arrived, early, begin, sums = [], [], 0, []
    for number, pairs in enumerate(sent_order(columns)):
        end = begin + len(pairs)
        sums, parts = lax.optimization_barrier((sums, parts))
        places, earlier = (begin, end), parts[begin:end]
        if number == 0:
            right, *earlier = made(chips - 1, places, left, [blocks], earlier, keep=True)
            right, *sums = made(chips, places, left, [right, crossed], earlier, keep=True)
        else:
            if pairs == [0]:
                earlier = [*earlier, *early]
            work = 5_000_000_000 if pairs == [0] else 1_000_000
            sums = made(chips - 1, places, left, [right], earlier, work=work)
        for pair, part in zip(pairs, sums):
            across = [(device, device ^ pair) for device in range(columns)]
            moved = lax.ppermute(part, "col", across) if pair else part
            (arrived if number else early).append(moved)
        begin = end

    vmem = pl.BlockSpec(memory_space=pltpu.VMEM)
    owned = pl.pallas_call(
        last_kernel,
        in_specs=[vmem] * len(arrived),
        out_specs=vmem,
        out_shape=jax.ShapeDtypeStruct((SC * HALF, LANES), jnp.float32),
        scratch_shapes=[pltpu.VMEM((LANES, LANES), jnp.float32)],
        compiler_params=pltpu.CompilerParams(vmem_limit_bytes=16 * MIB),
    )(*arrived)
    return blocks_view(owned)[None]


def solution(mesh):
    columns, rows = mesh.shape["col"], mesh.shape["row"]
    return jax.shard_map(
        functools.partial(per_device, columns, rows),
        mesh=mesh,
        in_specs=(P(("groups", "col"), "row", None), P(("groups", "col"), "row", None, None)),
        out_specs=P(("groups", "row"), "col", None),
        check_vma=False,
    )
```
